768 devices in a mesh: blk: 12 (over z_lo, core), col: 64 (over y, x, z_hi).
Axes of the slice: x: 4, y: 8, z: 12 (z_hi: 2, z_lo: 6; z = z_hi * 6 + z_lo), core: 2. Of those that a mesh axis runs over, the one named last changes fastest.
Arguments:
- amplitudes: bfloat16 [2304, 1, 3072], P('blk', None, 'col'), may hold values from -6 to 6
- integrals: bfloat16 [1, 3072, 3072], P(None, 'col', 'blk'), may hold values from -0.109375 to 0.109375
Outputs:
- ladder_residual: float32 [2304, 1, 3072], P('col', None, 'blk')
The draws below stay inside these ranges and needn't reach their ends.
All inputs are finite; a program needn't handle non-finite values.
Results may differ from the reference program's by a relative error of at most 0.0003.
Values may be sent and summed in bfloat16 or wider, within the bound.
A program may use at most 32 MiB of HBM per device.

```python
import jax
import jax.numpy as jnp

IRW = 1
PAIRS = 3072
OIJ = 2304


def block_scale(own_key, extent, cuts, low, high):
    factor_of = 1.0
    for dim, shards_of in cuts:
        draws = jax.random.uniform(jax.random.fold_in(jax.random.fold_in(own_key, 6), dim), (shards_of,), jnp.float32, low / len(cuts), high / len(cuts))
        factor_of = factor_of * jnp.repeat(jnp.exp(draws), extent[dim] // shards_of).reshape((-1,) + (1,) * (len(extent) - 1 - dim))
    return factor_of


def noise(key, shape, deviation, reach, cuts=(), kind=jnp.bfloat16):
    entries = deviation * jax.random.normal(key, shape, jnp.float32)
    if cuts:
        entries = entries * block_scale(key, shape, cuts, -0.22, 0.18)
    return jnp.clip(entries, -reach, reach).astype(kind)


def setup_inputs(seed: int = 0) -> dict:
    key_list = jax.random.split(jax.random.key(seed), 3)
    amplitudes = noise(key_list[0], (OIJ, IRW, PAIRS), 1.0, 6.0, ((0, 12), (2, 64)))
    integrals = noise(key_list[1], (IRW, PAIRS, PAIRS), PAIRS ** -0.5, 0.109375, ((1, 64), (2, 12)))
    return dict(amplitudes=amplitudes, integrals=integrals)


def reference(amplitudes, integrals):
    amps_wide = amplitudes.astype(jnp.float32)

    def one_irrep(block):
        left = amps_wide[:, block, :]
        right = integrals[block].astype(jnp.float32)
        return jnp.dot(left, right, preferred_element_type=jnp.float32)

    blocks = [one_irrep(block) for block in range(IRW)]
    ladder_sum = jnp.stack(blocks, axis=1)
    return 0.5 * ladder_sum
```

```python
import functools

import jax
import jax.numpy as jnp
from jax import lax
from jax.experimental import pallas as pl
from jax.experimental.pallas import tpu as pltpu
from jax.sharding import PartitionSpec as P

MESH = pl.DeviceIdType.MESH
NX, NY, NZ = 4, 8, 6


def device(y, x, zh, zl, core):
    return {"blk": zl * 2 + core, "col": (y * NX + x) * 2 + zh}


def remote(src, dst, send, recv, where):
    return pltpu.make_async_remote_copy(
        src_ref=src, dst_ref=dst, send_sem=send, recv_sem=recv, device_id=where, device_id_type=MESH
    )


def kernel(
    a_ref, b_ref, out_ref,
    a_own, a_line, a_whole, a_half, b_all, part, near, far, total,
    local_sem, line_send, line_recv, row_send, row_recv, pair_send, pair_recv,
    b_send, b_recv, near_send, near_recv, far_send, far_recv,
):
    blk, col = lax.axis_index("blk"), lax.axis_index("col")
    zl, core = blk // 2, blk % 2
    zh, x, y = col % 2, (col // 2) % NX, col // (2 * NX)
    at = functools.partial(device)

    load_a = pltpu.make_async_copy(a_ref, a_own, local_sem.at[0])
    load_b = pltpu.make_async_copy(b_ref, b_all.at[0], local_sem.at[1])
    load_a.start()
    load_b.start()

    barrier = pltpu.get_barrier_semaphore()

    def greet(where):
        pl.semaphore_signal(barrier, inc=1, device_id=where, device_id_type=MESH)

    greet(at(y, x, 1 - zh, zl, core))
    for d in range(1, NY):
        greet(at((y + d) % NY, x, zh, zl, core))
    for d in range(1, NZ):
        greet(at(y, x, zh, (zl + d) % NZ, core))
    for d in range(1, NX):
        greet(at(y, (x + d) % NX, zh, zl, core))
    greet(at(y, x, zh, zl, 1 - core))

    load_a.wait()
    mine = a_own[...]
    a_line[zl, 0] = mine[:, 0:128]
    a_line[zl, 1] = jnp.concatenate([mine[:, 96:192], mine[:, 64:96]], axis=1)
    pl.semaphore_wait(barrier, NY + NZ + NX - 1)

    line = [
        remote(a_line.at[zl], a_line.at[zl], line_send.at[d], line_recv.at[d], at(y, x, zh, (zl + d) % NZ, core))
        for d in range(1, NZ)
    ]
    for copy in line:
        copy.start()
    ring = [
        remote(b_ref, b_all.at[d], b_send.at[d], b_recv.at[d], at((y + d) % NY, x, zh, zl, core))
        for d in range(1, NY)
    ]
    for copy in ring:
        copy.start()

    for copy in line:
        copy.wait_recv()

    def rows(d):
        to = (y + d) % NY
        pair, odd = to // 2, to % 2
        whole = remote(
            a_line.at[(3 * pair + 2 * odd) // 2], a_whole.at[d], row_send.at[d], row_recv.at[d], at(to, x, zh, zl, core)
        )
        half = remote(
            a_line.at[(3 * pair + 1) // 2, odd], a_half.at[d], row_send.at[d], row_recv.at[d], at(to, x, zh, zl, core)
        )
        return core == pair % 2, whole, half

    for d in range(1, NY):
        is_whole, whole, half = rows(d)

        @pl.when(is_whole)
        def _():
            whole.start()

        @pl.when(jnp.logical_not(is_whole))
        def _():
            half.start()

    odd = y % 2
    have_whole = core == (y // 2) % 2
    sibling = at(y, x, zh, zl, 1 - core)
    own_whole = a_line.at[(3 * (y // 2) + 2 * odd) // 2]
    own_half = a_line.at[(3 * (y // 2) + 1) // 2, odd]

    def give(buffer, own, d):
        return remote(own if d == 0 else buffer.at[d], buffer.at[d], pair_send.at[d], pair_recv.at[d], sibling)

    @pl.when(have_whole)
    def _():
        give(a_whole, own_whole, 0).start()
        a_whole[0] = own_whole[...]
        for d in range(1, NY):
            remote(own_whole, a_whole.at[d], row_send.at[d], row_recv.at[d], sibling).wait_recv()
            give(a_whole, own_whole, d).start()
        for d in range(NY):
            give(a_half, own_half, d).wait_recv()

    @pl.when(jnp.logical_not(have_whole))
    def _():
        give(a_half, own_half, 0).start()
        a_half[0] = own_half[...]
        for d in range(1, NY):
            remote(own_half, a_half.at[d], row_send.at[d], row_recv.at[d], sibling).wait_recv()
            give(a_half, own_half, d).start()
        for d in range(NY):
            give(a_whole, own_whole, d).wait_recv()

    load_b.wait()
    for copy in ring:
        copy.wait_recv()

    depth = NY * 48
    right = b_all[...].reshape(depth, 256)
    w0 = a_whole[:, 0].reshape(depth, 128)
    w1 = a_whole[:, 1].reshape(depth, 128)
    h = a_half[...].reshape(depth, 128)
    units = [jnp.where(odd == 1, h, w0), jnp.where(odd == 1, w0, w1), jnp.where(odd == 1, w1, h)]
    for j, unit in enumerate(units):
        value = lax.dot_general(unit, right, (((0,), (0,)), ((), ())), preferred_element_type=jnp.float32)
        row = 96 * j
        while row < 96 * (j + 1):
            block, offset = row // 36, row % 36
            count = min(36 - offset, 96 * (j + 1) - row)
            piece = value[row - 96 * j : row - 96 * j + count]
            part[block, offset : offset + count] = piece[:, 0:128]
            part[block, 36 + offset : 36 + offset + count] = piece[:, 128:256]
            row += count

    def to_near(kind, d):
        half_of = (1 - zh) if kind == 0 else zh
        to = (x + d) % NX
        return remote(
            part.at[to * 2 + half_of], near.at[kind, d], near_send.at[kind, d], near_recv.at[kind, d],
            at(y, to, zh, zl, core),
        )

    for kind in range(2):
        for d in range(1, NX):
            to_near(kind, d).start()
    for d in range(1, NX):
        to_near(0, d).wait_recv()
    total[0] = part[x * 2 + 1 - zh] + near[0, 1] + (near[0, 2] + near[0, 3])
    over = remote(total.at[0], far, far_send, far_recv, at(y, x, 1 - zh, zl, core))
    over.start()
    for d in range(1, NX):
        to_near(1, d).wait_recv()
    total[1] = part[x * 2 + zh] + near[1, 1] + (near[1, 2] + near[1, 3])
    over.wait_recv()
    result = 0.5 * (total[1] + far[...])
    out_ref[pl.ds(0, 36, stride=2), :] = result[0:36]
    out_ref[pl.ds(1, 36, stride=2), :] = result[36:72]

    over.wait_send()
    for kind in range(2):
        for d in range(1, NX):
            to_near(kind, d).wait_send()
    for copy in line + ring:
        copy.wait_send()
    for d in range(1, NY):
        is_whole, whole, half = rows(d)

        @pl.when(is_whole)
        def _():
            whole.wait_send()

        @pl.when(jnp.logical_not(is_whole))
        def _():
            half.wait_send()

    @pl.when(have_whole)
    def _():
        for d in range(NY):
            give(a_whole, own_whole, d).wait_send()

    @pl.when(jnp.logical_not(have_whole))
    def _():
        for d in range(NY):
            give(a_half, own_half, d).wait_send()


def body(amplitudes, integrals):
    left = jnp.transpose(amplitudes, (1, 2, 0)).reshape(48, 192)
    right = integrals.reshape(48, 256)
    dma = pltpu.SemaphoreType.DMA
    out = pl.pallas_call(
        kernel,
        out_shape=jax.ShapeDtypeStruct((72, 128), jnp.float32),
        in_specs=[pl.BlockSpec(memory_space=pl.ANY)] * 2,
        out_specs=pl.BlockSpec(memory_space=pltpu.VMEM),
        scratch_shapes=[
            pltpu.VMEM((48, 192), jnp.bfloat16),
            pltpu.VMEM((NZ, 2, 48, 128), jnp.bfloat16),
            pltpu.VMEM((NY, 2, 48, 128), jnp.bfloat16),
            pltpu.VMEM((NY, 48, 128), jnp.bfloat16),
            pltpu.VMEM((NY, 48, 256), jnp.bfloat16),
            pltpu.VMEM((8, 72, 128), jnp.float32),
            pltpu.VMEM((2, NX, 72, 128), jnp.float32),
            pltpu.VMEM((72, 128), jnp.float32),
            pltpu.VMEM((2, 72, 128), jnp.float32),
            dma((2,)), dma((NZ,)), dma((NZ,)), dma((NY,)), dma((NY,)), dma((NY,)), dma((NY,)),
            dma((NY,)), dma((NY,)), dma((2, NX)), dma((2, NX)), dma, dma,
        ],
        compiler_params=pltpu.CompilerParams(collective_id=0, has_side_effects=True),
    )(left, right)
    return out.reshape(36, 1, 256)


def solution(mesh):
    return jax.shard_map(
        body,
        mesh=mesh,
        in_specs=(P("blk", None, "col"), P(None, "col", "blk")),
        out_specs=P("col", None, "blk"),
        check_vma=False,
    )
```

```python
import jax
import jax.numpy as jnp
from jax import lax
from jax.experimental import pallas as pl
from jax.experimental.pallas import tpu as pltpu
from jax.sharding import PartitionSpec as P

MESH = pl.DeviceIdType.MESH
NX, NY, NL, NZ = 4, 8, 6, 12
RING_Y = (4, 3, 5, 2, 6, 1, 7)


def device(y, x, z, core):
    return {"blk": (z % NL) * 2 + core, "col": (y * NX + x) * 2 + z // NL}


def remote(src, dst, send, recv, where):
    return pltpu.make_async_remote_copy(
        src_ref=src, dst_ref=dst, send_sem=send, recv_sem=recv, device_id=where, device_id_type=MESH
    )


def chosen(block, wide, to, half):
    lane = lax.broadcasted_iota(jnp.int32, (192, 128), 1)
    row = lax.broadcasted_iota(jnp.int32, (192, 128), 0)
    slot = (lane >= 40).astype(jnp.int32) + (lane >= 80).astype(jnp.int32) + (lane >= 120).astype(jnp.int32)
    inner = lane - 40 * slot
    odd = to % 2
    first = jnp.where(wide, odd, 2 - 2 * odd)
    slots = jnp.where(wide, 3, 2)
    source = 288 * to - 192 * block + 36 * half + 72 * (slot + first) + inner
    hit = (source == row) & (inner < 36) & (slot < slots)
    return jnp.where(hit, 1.0, 0.0).astype(jnp.bfloat16)


def kernel(
    a_ref, b_ref, out_ref,
    a_own, tiles, a_all, b_all, part, near,
    local_sem, tile_send, tile_recv, pair_send, pair_recv,
    own_send, own_recv, far_send, far_recv, near_send, near_recv, answer, answer_far,
):
    blk, col = lax.axis_index("blk"), lax.axis_index("col")
    zl, core = blk // 2, blk % 2
    zh, x, y = col % 2, (col // 2) % NX, col // (2 * NX)
    z = zh * NL + zl
    slot, other = zh * NY + y, (1 - zh) * NY + y

    load_a = pltpu.make_async_copy(a_ref, a_own, local_sem.at[0])
    load_b = pltpu.make_async_copy(b_ref, b_all.at[slot], local_sem.at[1])
    load_a.start()
    load_b.start()

    split = blk % 3 == 1
    targets = (2 * (blk // 3) + (blk % 3) // 2, 2 * (blk // 3) + 1)
    pair = y // 2
    kind = jnp.where(core == pair % 2, 0, 1)
    giver = jnp.where(kind == 0, (3 * pair + 2 * (y % 2)) // 2, (3 * pair + 1) // 2)
    gives_self = zl == giver
    sent_kind = jnp.where(split, 1, 0)
    sibling = device(y, x, z, 1 - core)

    barrier = pltpu.get_barrier_semaphore()

    def greet(where):
        pl.semaphore_signal(barrier, inc=1, device_id=where, device_id_type=MESH)

    def providers():
        for half in (0, 1):
            at = half * NL + giver
            for d in range(NY):
                yield at, device((y + d) % NY, x, at, core)

    def signal(sem, where):
        pl.semaphore_signal(sem, inc=1, device_id=where, device_id_type=MESH)

    for d in RING_Y:
        greet(device((y + d) % NY, x, z, core))
    for d in range(1, NX):
        greet(device(y, (x + d) % NX, z, core))
    greet(sibling)
    for at, where in providers():

        @pl.when(at > z)
        def _():
            greet(where)

    for to in range(1, NZ):

        @pl.when(to > z)
        def _():
            greet(device(targets[0], x, to, core))

        @pl.when((to > z) & split)
        def _():
            greet(device(targets[1], x, to, core))

    @pl.when(z < NL)
    def _():
        greet(device(y, x, z + NL, core))

    load_a.wait()
    mine = a_own[...]

    def make(k, half):
        wide = jnp.logical_not(split)
        tile = jnp.dot(mine, chosen(blk, wide, targets[k], half), preferred_element_type=jnp.float32)
        tiles[k, half] = tile.astype(jnp.bfloat16)

    make(0, 0)
    make(0, 1)

    @pl.when(split)
    def _():
        make(1, 0)
        make(1, 1)

    per_plane = jnp.where(split, 2, 1)
    lower = jnp.where(giver < z, 1, 0) + jnp.where(NL + giver < z, 1, 0)
    partners = (NY - 1) + (NX - 1) + 1 + per_plane * z + NY * lower + jnp.where(z >= NL, 1, 0)
    pl.semaphore_wait(barrier, partners)

    across = remote(b_ref, b_all.at[slot], far_send.at[0], far_recv.at[0], device(y, x, (z + NL) % NZ, core))

    @pl.when(z >= NL)
    def _():
        signal(answer_far, device(y, x, z - NL, core))
        across.start()

    for at, where in providers():

        @pl.when(at < z)
        def _():
            signal(answer.at[z], where)

    def tile_copy(k, to):
        return remote(
            tiles.at[k, to // NL], a_all.at[sent_kind, slot], tile_send.at[k, to], tile_recv.at[slot],
            device(targets[k], x, to, core),
        )

    def each_tile(to, act):
        @pl.when((to != z) | (targets[0] != y))
        def _():
            act(tile_copy(0, to))

        @pl.when(split & ((to != z) | (targets[1] != y)))
        def _():
            act(tile_copy(1, to))

    def start_tiles(planes, low):
        for to in planes:

            @pl.when(to <= z if low else to > z)
            def _():
                if not low:
                    pl.semaphore_wait(answer.at[to], per_plane)
                each_tile(to, lambda copy: copy.start())

    start_tiles(range(NZ), True)

    own = [
        remote(b_ref, b_all.at[slot], own_send.at[d], own_recv.at[d], device((y + d) % NY, x, z, core))
        for d in RING_Y
    ]
    for copy in own:
        copy.start()
    start_tiles(range(1, NL), False)

    @pl.when(z < NL)
    def _():
        pl.semaphore_wait(answer_far, 1)
        across.start()

    @pl.when(gives_self)
    def _():
        a_all[kind, slot] = tiles[jnp.where(split & (targets[1] == y), 1, 0), zh]

    across.wait_recv()
    rest = [
        remote(b_all.at[other], b_all.at[other], far_send.at[d], far_recv.at[d], device((y + d) % NY, x, z, core))
        for d in RING_Y
    ]
    for copy in rest:
        copy.start()

    start_tiles(range(NL, NZ), False)

    def arrival(s):
        return remote(a_all.at[kind, s], a_all.at[kind, s], tile_send.at[0, 0], tile_recv.at[s], sibling)

    def give(s):
        return remote(a_all.at[kind, s], a_all.at[kind, s], pair_send.at[s], pair_recv.at[s], sibling)

    def take(s):
        return remote(a_all.at[1 - kind, s], a_all.at[1 - kind, s], pair_send.at[s], pair_recv.at[s], sibling)

    @pl.when(jnp.logical_not(gives_self))
    def _():
        arrival(slot).wait_recv()

    give(slot).start()
    for d in range(1, NY):
        s = zh * NY + (y + d) % NY
        arrival(s).wait_recv()
        give(s).start()
    for d in range(NY):
        s = (1 - zh) * NY + (y + d) % NY
        arrival(s).wait_recv()
        give(s).start()
    for s in range(2 * NY):
        take(s).wait_recv()

    load_b.wait()
    for copy in own:
        copy.wait_recv()

    depth = NY * 48

    def product(k, base):
        left = a_all[k, pl.ds(base, NY)].reshape(depth, 128)
        right = b_all[pl.ds(base, NY)].reshape(depth, 256)
        return lax.dot_general(left, right, (((0,), (0,)), ((), ())), preferred_element_type=jnp.float32)

    base, far_base = zh * NY, (1 - zh) * NY
    wide, narrow = product(0, base), product(1, base)
    for copy in rest:
        copy.wait_recv()
    wide += product(0, far_base)
    narrow += product(1, far_base)
    w = [wide[40 * i : 40 * i + 36] for i in range(3)]
    n = [narrow[40 * i : 40 * i + 36] for i in range(2)]
    odd = y % 2 == 1
    sums = (
        jnp.where(odd, n[0], w[0]),
        jnp.where(odd, n[1] + w[0], w[1]),
        jnp.where(odd, w[1], w[2] + n[0]),
        jnp.where(odd, w[2], n[1]),
    )
    for i, value in enumerate(sums):
        part[i, 0:36] = value[:, 0:128]
        part[i, 36:72] = value[:, 128:256]

    gather = []
    for d in (2, 1, 3):
        to = (x + d) % NX
        gather.append(remote(part.at[to], near.at[d], near_send.at[d], near_recv.at[d], device(y, to, z, core)))
    for copy in gather:
        copy.start()
    for copy in gather:
        copy.wait_recv()
    result = 0.5 * ((part[x] + near[1]) + (near[2] + near[3]))
    out_ref[pl.ds(0, 36, stride=2), :] = result[0:36]
    out_ref[pl.ds(1, 36, stride=2), :] = result[36:72]

    across.wait_send()
    for to in range(NZ):
        each_tile(to, lambda copy: copy.wait_send())
    for s in range(2 * NY):
        give(s).wait_send()
    for copy in own + rest + gather:
        copy.wait_send()


def body(amplitudes, integrals):
    left = jnp.transpose(amplitudes, (1, 2, 0)).reshape(48, 192)
    right = integrals.reshape(48, 256)
    dma = pltpu.SemaphoreType.DMA
    out = pl.pallas_call(
        kernel,
        out_shape=jax.ShapeDtypeStruct((72, 128), jnp.float32),
        in_specs=[pl.BlockSpec(memory_space=pl.ANY)] * 2,
        out_specs=pl.BlockSpec(memory_space=pltpu.VMEM),
        scratch_shapes=[
            pltpu.VMEM((48, 192), jnp.bfloat16),
            pltpu.VMEM((2, 2, 48, 128), jnp.bfloat16),
            pltpu.VMEM((2, 2 * NY, 48, 128), jnp.bfloat16),
            pltpu.VMEM((2 * NY, 48, 256), jnp.bfloat16),
            pltpu.VMEM((NX, 72, 128), jnp.float32),
            pltpu.VMEM((NX, 72, 128), jnp.float32),
            dma((2,)), dma((2, NZ)), dma((2 * NY,)), dma((2 * NY,)), dma((2 * NY,)),
            dma((NY,)), dma((NY,)), dma((NY,)), dma((NY,)), dma((NX,)), dma((NX,)),
            pltpu.SemaphoreType.REGULAR((NZ,)), pltpu.SemaphoreType.REGULAR,
        ],
        compiler_params=pltpu.CompilerParams(collective_id=0, has_side_effects=True),
    )(left, right)
    return out.reshape(36, 1, 256)


def solution(mesh):
    return jax.shard_map(
        body,
        mesh=mesh,
        in_specs=(P("blk", None, "col"), P(None, "col", "blk")),
        out_specs=P("col", None, "blk"),
        check_vma=False,
    )
```

```python
import jax
import jax.numpy as jnp
from jax import lax
from jax.experimental import pallas as pl
from jax.experimental.pallas import tpu as pltpu
from jax.sharding import PartitionSpec as P

MESH = pl.DeviceIdType.MESH
NX, NY, NL, NZ = 4, 8, 6, 12
RING_Y = (4, 3, 5, 2, 6, 1, 7)


def device(y, x, z, core):
    return {"blk": (z % NL) * 2 + core, "col": (y * NX + x) * 2 + z // NL}


def remote(src, dst, send, recv, where):
    return pltpu.make_async_remote_copy(
        src_ref=src, dst_ref=dst, send_sem=send, recv_sem=recv, device_id=where, device_id_type=MESH
    )


def chosen(block, wide, to, half):
    lane = lax.broadcasted_iota(jnp.int32, (192, 128), 1)
    row = lax.broadcasted_iota(jnp.int32, (192, 128), 0)
    slot = (lane >= 40).astype(jnp.int32) + (lane >= 80).astype(jnp.int32) + (lane >= 120).astype(jnp.int32)
    inner = lane - 40 * slot
    odd = to % 2
    first = jnp.where(wide, odd, 2 - 2 * odd)
    slots = jnp.where(wide, 3, 2)
    source = 288 * to - 192 * block + 36 * half + 72 * (slot + first) + inner
    hit = (source == row) & (inner < 36) & (slot < slots)
    return jnp.where(hit, 1.0, 0.0).astype(jnp.bfloat16)


def kernel(
    a_ref, b_ref, out_ref,
    a_own, tiles, a_all, b_all, part, near,
    local_sem, tile_send, tile_recv, pair_send, pair_recv,
    own_send, own_recv, far_send, far_recv, near_send, near_recv, answer, answer_far, answer_y, answer_x,
):
    blk, col = lax.axis_index("blk"), lax.axis_index("col")
    zl, core = blk // 2, blk % 2
    zh, x, y = col % 2, (col // 2) % NX, col // (2 * NX)
    z = zh * NL + zl
    slot, other = zh * NY + y, (1 - zh) * NY + y

    load_a = pltpu.make_async_copy(a_ref, a_own, local_sem.at[0])
    load_b = pltpu.make_async_copy(b_ref, b_all.at[slot], local_sem.at[1])
    load_a.start()
    load_b.start()

    split = blk % 3 == 1
    targets = (2 * (blk // 3) + (blk % 3) // 2, 2 * (blk // 3) + 1)
    pair = y // 2
    kind = jnp.where(core == pair % 2, 0, 1)
    giver = jnp.where(kind == 0, (3 * pair + 2 * (y % 2)) // 2, (3 * pair + 1) // 2)
    gives_self = zl == giver
    sent_kind = jnp.where(split, 1, 0)
    sibling = device(y, x, z, 1 - core)

    barrier = pltpu.get_barrier_semaphore()

    def greet(where):
        pl.semaphore_signal(barrier, inc=1, device_id=where, device_id_type=MESH)

    def providers():
        for half in (0, 1):
            at = half * NL + giver
            for d in range(NY):
                yield at, device((y + d) % NY, x, at, core)

    def signal(sem, where):
        pl.semaphore_signal(sem, inc=1, device_id=where, device_id_type=MESH)

    def rank(at):
        return jnp.where(at < 4, at, 11 - at)

    for d in range(1, NX):

        @pl.when((x + d) % NX > x)
        def _():
            greet(device(y, (x + d) % NX, z, core))

    for d in RING_Y:

        @pl.when(rank((y + d) % NY) > rank(y))
        def _():
            greet(device((y + d) % NY, x, z, core))

    greet(sibling)
    for at, where in providers():

        @pl.when(at > z)
        def _():
            greet(where)

    for to in range(1, NZ):

        @pl.when(to > z)
        def _():
            greet(device(targets[0], x, to, core))

        @pl.when((to > z) & split)
        def _():
            greet(device(targets[1], x, to, core))

    @pl.when(z < NL)
    def _():
        greet(device(y, x, z + NL, core))

    per_plane = jnp.where(split, 2, 1)
    lower = jnp.where(giver < z, 1, 0) + jnp.where(NL + giver < z, 1, 0)
    partners = rank(y) + x + 1 + per_plane * z + NY * lower + jnp.where(z >= NL, 1, 0)
    pl.semaphore_wait(barrier, partners)

    across = remote(b_ref, b_all.at[slot], far_send.at[0], far_recv.at[0], device(y, x, (z + NL) % NZ, core))

    @pl.when(z >= NL)
    def _():
        signal(answer_far, device(y, x, z - NL, core))
        across.start()

    for at, where in providers():

        @pl.when(at < z)
        def _():
            signal(answer.at[z], where)

    for d in range(1, NY):

        @pl.when(rank((y + d) % NY) < rank(y))
        def _():
            signal(answer_y.at[NY - d], device((y + d) % NY, x, z, core))

    for d in range(1, NX):

        @pl.when((x + d) % NX < x)
        def _():
            signal(answer_x.at[NX - d], device(y, (x + d) % NX, z, core))

    load_a.wait()
    mine = a_own[...]

    def make(k, half):
        wide = jnp.logical_not(split)
        tile = jnp.dot(mine, chosen(blk, wide, targets[k], half), preferred_element_type=jnp.float32)
        tiles[k, half] = tile.astype(jnp.bfloat16)

    make(0, 0)
    make(0, 1)

    @pl.when(split)
    def _():
        make(1, 0)
        make(1, 1)

    def tile_copy(k, to):
        return remote(
            tiles.at[k, to // NL], a_all.at[sent_kind, slot], tile_send.at[k, to], tile_recv.at[slot],
            device(targets[k], x, to, core),
        )

    def each_tile(to, act):
        @pl.when((to != z) | (targets[0] != y))
        def _():
            act(tile_copy(0, to))

        @pl.when(split & ((to != z) | (targets[1] != y)))
        def _():
            act(tile_copy(1, to))

    def start_tiles(planes, low):
        for to in planes:

            @pl.when(to < z if low else to > z)
            def _():
                if not low:
                    pl.semaphore_wait(answer.at[to], per_plane)
                each_tile(to, lambda copy: copy.start())

    start_tiles(range(NZ - 1), True)
    for d in RING_Y:

        @pl.when(rank((y + d) % NY) > rank(y))
        def _():
            pl.semaphore_wait(answer_y.at[d], 1)

    own = [
        remote(b_ref, b_all.at[slot], own_send.at[d], own_recv.at[d], device((y + d) % NY, x, z, core))
        for d in RING_Y
    ]
    for copy in own:
        copy.start()
    each_tile(z, lambda copy: copy.start())
    start_tiles(range(1, NL), False)

    @pl.when(z < NL)
    def _():
        pl.semaphore_wait(answer_far, 1)
        across.start()

    @pl.when(gives_self)
    def _():
        a_all[kind, slot] = tiles[jnp.where(split & (targets[1] == y), 1, 0), zh]

    across.wait_recv()
    rest = [
        remote(b_all.at[other], b_all.at[other], far_send.at[d], far_recv.at[d], device((y + d) % NY, x, z, core))
        for d in RING_Y
    ]
    for copy in rest:
        copy.start()

    start_tiles(range(NL, NZ), False)

    def arrival(s):
        return remote(a_all.at[kind, s], a_all.at[kind, s], tile_send.at[0, 0], tile_recv.at[s], sibling)

    def give(s):
        return remote(a_all.at[kind, s], a_all.at[kind, s], pair_send.at[s], pair_recv.at[s], sibling)

    def take(s):
        return remote(a_all.at[1 - kind, s], a_all.at[1 - kind, s], pair_send.at[s], pair_recv.at[s], sibling)

    @pl.when(jnp.logical_not(gives_self))
    def _():
        arrival(slot).wait_recv()

    give(slot).start()
    for d in range(1, NY):
        s = zh * NY + (y + d) % NY
        arrival(s).wait_recv()
        give(s).start()
    for d in range(NY):
        s = (1 - zh) * NY + (y + d) % NY
        arrival(s).wait_recv()
        give(s).start()
    for s in range(2 * NY):
        take(s).wait_recv()

    load_b.wait()
    for copy in own:
        copy.wait_recv()

    depth = NY * 48

    def product(k, base):
        left = a_all[k, pl.ds(base, NY)].reshape(depth, 128)
        right = b_all[pl.ds(base, NY)].reshape(depth, 256)
        return lax.dot_general(left, right, (((0,), (0,)), ((), ())), preferred_element_type=jnp.float32)

    base, far_base = zh * NY, (1 - zh) * NY
    wide, narrow = product(0, base), product(1, base)
    for copy in rest:
        copy.wait_recv()
    wide += product(0, far_base)
    narrow += product(1, far_base)
    w = [wide[40 * i : 40 * i + 36] for i in range(3)]
    n = [narrow[40 * i : 40 * i + 36] for i in range(2)]
    odd = y % 2 == 1
    sums = (
        jnp.where(odd, n[0], w[0]),
        jnp.where(odd, n[1] + w[0], w[1]),
        jnp.where(odd, w[1], w[2] + n[0]),
        jnp.where(odd, w[2], n[1]),
    )
    for i, value in enumerate(sums):
        part[i, 0:36] = value[:, 0:128]
        part[i, 36:72] = value[:, 128:256]

    for d in range(1, NX):

        @pl.when((x + d) % NX > x)
        def _():
            pl.semaphore_wait(answer_x.at[d], 1)

    gather = []
    for d in (2, 1, 3):
        to = (x + d) % NX
        gather.append(remote(part.at[to], near.at[d], near_send.at[d], near_recv.at[d], device(y, to, z, core)))
    for copy in gather:
        copy.start()
    for copy in gather:
        copy.wait_recv()
    result = 0.5 * ((part[x] + near[1]) + (near[2] + near[3]))
    out_ref[pl.ds(0, 36, stride=2), :] = result[0:36]
    out_ref[pl.ds(1, 36, stride=2), :] = result[36:72]

    across.wait_send()
    for to in range(NZ):
        each_tile(to, lambda copy: copy.wait_send())
    for s in range(2 * NY):
        give(s).wait_send()
    for copy in own + rest + gather:
        copy.wait_send()


def body(amplitudes, integrals):
    left = jnp.transpose(amplitudes, (1, 2, 0)).reshape(48, 192)
    right = integrals.reshape(48, 256)
    dma = pltpu.SemaphoreType.DMA
    out = pl.pallas_call(
        kernel,
        out_shape=pltpu.VMEM((72, 128), jnp.float32),
        in_specs=[pl.BlockSpec(memory_space=pl.ANY)] * 2,
        out_specs=pl.BlockSpec(memory_space=pltpu.VMEM),
        scratch_shapes=[
            pltpu.VMEM((48, 192), jnp.bfloat16),
            pltpu.VMEM((2, 2, 48, 128), jnp.bfloat16),
            pltpu.VMEM((2, 2 * NY, 48, 128), jnp.bfloat16),
            pltpu.VMEM((2 * NY, 48, 256), jnp.bfloat16),
            pltpu.VMEM((NX, 72, 128), jnp.float32),
            pltpu.VMEM((NX, 72, 128), jnp.float32),
            dma((2,)), dma((2, NZ)), dma((2 * NY,)), dma((2 * NY,)), dma((2 * NY,)),
            dma((NY,)), dma((NY,)), dma((NY,)), dma((NY,)), dma((NX,)), dma((NX,)),
            pltpu.SemaphoreType.REGULAR((NZ,)), pltpu.SemaphoreType.REGULAR,
            pltpu.SemaphoreType.REGULAR((NY,)), pltpu.SemaphoreType.REGULAR((NX,)),
        ],
        compiler_params=pltpu.CompilerParams(collective_id=0, has_side_effects=True),
    )(left, right)
    return out.reshape(36, 1, 256)


def solution(mesh):
    return jax.shard_map(
        body,
        mesh=mesh,
        in_specs=(P("blk", None, "col"), P(None, "col", "blk")),
        out_specs=P("col", None, "blk"),
        check_vma=False,
    )
```

```python
import jax
import jax.numpy as jnp
from jax import lax
from jax.experimental import pallas as pl
from jax.experimental.pallas import tpu as pltpu
from jax.sharding import PartitionSpec as P

MESH = pl.DeviceIdType.MESH
NX, NY, NL, NZ = 4, 8, 6, 12
RING_Y = (4, 3, 5, 2, 6, 1, 7)
ORDER_Y = (0, 1, 2, 3, 7, 6, 5, 4)


def device(y, x, z, core):
    return {"blk": (z % NL) * 2 + core, "col": (y * NX + x) * 2 + z // NL}


def remote(src, dst, send, recv, where):
    return pltpu.make_async_remote_copy(
        src_ref=src, dst_ref=dst, send_sem=send, recv_sem=recv, device_id=where, device_id_type=MESH
    )


def chosen(block, wide, to, half):
    lane = lax.broadcasted_iota(jnp.int32, (192, 128), 1)
    row = lax.broadcasted_iota(jnp.int32, (192, 128), 0)
    slot = (lane >= 40).astype(jnp.int32) + (lane >= 80).astype(jnp.int32) + (lane >= 120).astype(jnp.int32)
    inner = lane - 40 * slot
    odd = to % 2
    first = jnp.where(wide, odd, 2 - 2 * odd)
    slots = jnp.where(wide, 3, 2)
    source = 288 * to - 192 * block + 36 * half + 72 * (slot + first) + inner
    hit = (source == row) & (inner < 36) & (slot < slots)
    return jnp.where(hit, 1.0, 0.0).astype(jnp.bfloat16)


def kernel(
    a_ref, b_ref, out_ref,
    a_own, tiles, a_all, b_all, part, near,
    local_sem, tile_send, tile_recv, pair_send, pair_recv,
    own_send, own_recv, rest_send, rest_recv, far_send, far_recv, near_send, near_recv, answer, answer_far, answer_y, answer_x,
):
    blk, col = lax.axis_index("blk"), lax.axis_index("col")
    zl, core = blk // 2, blk % 2
    zh, x, y = col % 2, (col // 2) % NX, col // (2 * NX)
    z = zh * NL + zl
    slot, other = zh * NY + y, (1 - zh) * NY + y

    load_a = pltpu.make_async_copy(a_ref, a_own, local_sem.at[0])
    load_b = pltpu.make_async_copy(b_ref, b_all.at[slot], local_sem.at[1])
    load_a.start()
    load_b.start()

    split = blk % 3 == 1
    targets = (2 * (blk // 3) + (blk % 3) // 2, 2 * (blk // 3) + 1)
    pair = y // 2
    kind = jnp.where(core == pair % 2, 0, 1)
    giver = jnp.where(kind == 0, (3 * pair + 2 * (y % 2)) // 2, (3 * pair + 1) // 2)
    gives_self = zl == giver
    sent_kind = jnp.where(split, 1, 0)
    sibling = device(y, x, z, 1 - core)

    barrier = pltpu.get_barrier_semaphore()

    def greet(where):
        pl.semaphore_signal(barrier, inc=1, device_id=where, device_id_type=MESH)

    def providers():
        for half in (0, 1):
            at = half * NL + giver
            for d in range(NY):
                yield at, device((y + d) % NY, x, at, core)

    def signal(sem, where):
        pl.semaphore_signal(sem, inc=1, device_id=where, device_id_type=MESH)

    def rank(at):
        return jnp.where(at < 4, at, 11 - at)

    for d in range(1, NX):

        @pl.when((x + d) % NX > x)
        def _():
            greet(device(y, (x + d) % NX, z, core))

    for d in RING_Y:

        @pl.when(rank((y + d) % NY) > rank(y))
        def _():
            greet(device((y + d) % NY, x, z, core))

    greet(sibling)
    for at, where in providers():

        @pl.when(at > z)
        def _():
            greet(where)

    for to in range(1, NZ):

        @pl.when(to > z)
        def _():
            greet(device(targets[0], x, to, core))

        @pl.when((to > z) & split)
        def _():
            greet(device(targets[1], x, to, core))

    @pl.when(z < NL)
    def _():
        greet(device(y, x, z + NL, core))

    per_plane = jnp.where(split, 2, 1)
    lower = jnp.where(giver < z, 1, 0) + jnp.where(NL + giver < z, 1, 0)
    partners = rank(y) + x + 1 + per_plane * z + NY * lower + jnp.where(z >= NL, 1, 0)
    pl.semaphore_wait(barrier, partners)

    across = remote(b_ref, b_all.at[slot], far_send.at[0], far_recv.at[0], device(y, x, (z + NL) % NZ, core))

    @pl.when(z >= NL)
    def _():
        signal(answer_far, device(y, x, z - NL, core))
        across.start()

    for at, where in providers():

        @pl.when(at < z)
        def _():
            signal(answer.at[z], where)

    for d in range(1, NY):

        @pl.when(rank((y + d) % NY) < rank(y))
        def _():
            signal(answer_y.at[NY - d], device((y + d) % NY, x, z, core))

    for d in range(1, NX):

        @pl.when((x + d) % NX < x)
        def _():
            signal(answer_x.at[NX - d], device(y, (x + d) % NX, z, core))

    load_a.wait()
    mine = a_own[...]

    def make(k, half):
        wide = jnp.logical_not(split)
        tile = jnp.dot(mine, chosen(blk, wide, targets[k], half), preferred_element_type=jnp.float32)
        tiles[k, half] = tile.astype(jnp.bfloat16)

    make(0, 0)
    make(0, 1)

    @pl.when(split)
    def _():
        make(1, 0)
        make(1, 1)

    def tile_copy(k, to):
        return remote(
            tiles.at[k, to // NL], a_all.at[sent_kind, slot], tile_send.at[k, to], tile_recv.at[slot],
            device(targets[k], x, to, core),
        )

    def each_tile(to, act):
        @pl.when((to != z) | (targets[0] != y))
        def _():
            act(tile_copy(0, to))

        @pl.when(split & ((to != z) | (targets[1] != y)))
        def _():
            act(tile_copy(1, to))

    def start_tiles(planes, low):
        for to in planes:

            @pl.when(to < z if low else to > z)
            def _():
                if not low:
                    pl.semaphore_wait(answer.at[to], per_plane)
                each_tile(to, lambda copy: copy.start())

    start_tiles(range(NZ - 1), True)
    for d in RING_Y:

        @pl.when(rank((y + d) % NY) > rank(y))
        def _():
            pl.semaphore_wait(answer_y.at[d], 1)

    def round_y(src, into, send, recv, act):
        for to in ORDER_Y:

            @pl.when(to != y)
            def _():
                act(remote(src, b_all.at[into], send.at[to], recv.at[y], device(to, x, z, core)))

    def own_copies(act):
        round_y(b_ref, slot, own_send, own_recv, act)

    def rest_copies(act):
        round_y(b_all.at[other], other, rest_send, rest_recv, act)

    def from_y(half, recv):
        for d in range(1, NY):
            at = (y + d) % NY
            block = b_all.at[half * NY + at]
            remote(block, block, own_send.at[0], recv.at[at], sibling).wait_recv()

    own_copies(lambda copy: copy.start())
    each_tile(z, lambda copy: copy.start())
    start_tiles(range(1, NL), False)

    @pl.when(z < NL)
    def _():
        pl.semaphore_wait(answer_far, 1)
        across.start()

    @pl.when(gives_self)
    def _():
        a_all[kind, slot] = tiles[jnp.where(split & (targets[1] == y), 1, 0), zh]

    across.wait_recv()
    rest_copies(lambda copy: copy.start())

    start_tiles(range(NL, NZ), False)

    def arrival(s):
        return remote(a_all.at[kind, s], a_all.at[kind, s], tile_send.at[0, 0], tile_recv.at[s], sibling)

    def give(s):
        return remote(a_all.at[kind, s], a_all.at[kind, s], pair_send.at[s], pair_recv.at[s], sibling)

    def take(s):
        return remote(a_all.at[1 - kind, s], a_all.at[1 - kind, s], pair_send.at[s], pair_recv.at[s], sibling)

    @pl.when(jnp.logical_not(gives_self))
    def _():
        arrival(slot).wait_recv()

    give(slot).start()
    for d in range(1, NY):
        s = zh * NY + (y + d) % NY
        arrival(s).wait_recv()
        give(s).start()
    for d in range(NY):
        s = (1 - zh) * NY + (y + d) % NY
        arrival(s).wait_recv()
        give(s).start()
    for s in range(2 * NY):
        take(s).wait_recv()

    load_b.wait()
    from_y(zh, own_recv)

    depth = NY * 48

    def product(k, base):
        left = a_all[k, pl.ds(base, NY)].reshape(depth, 128)
        right = b_all[pl.ds(base, NY)].reshape(depth, 256)
        return lax.dot_general(left, right, (((0,), (0,)), ((), ())), preferred_element_type=jnp.float32)

    base, far_base = zh * NY, (1 - zh) * NY
    wide, narrow = product(0, base), product(1, base)
    from_y(1 - zh, rest_recv)
    wide += product(0, far_base)
    narrow += product(1, far_base)
    w = [wide[40 * i : 40 * i + 36] for i in range(3)]
    n = [narrow[40 * i : 40 * i + 36] for i in range(2)]
    odd = y % 2 == 1
    sums = (
        jnp.where(odd, n[0], w[0]),
        jnp.where(odd, n[1] + w[0], w[1]),
        jnp.where(odd, w[1], w[2] + n[0]),
        jnp.where(odd, w[2], n[1]),
    )
    for i, value in enumerate(sums):
        part[i, 0:36] = value[:, 0:128]
        part[i, 36:72] = value[:, 128:256]

    for d in range(1, NX):

        @pl.when((x + d) % NX > x)
        def _():
            pl.semaphore_wait(answer_x.at[d], 1)

    def sums_x(act):
        for to in range(NX):
            d = jnp.where(to > x, to - x, to - x + NX)

            @pl.when(to != x)
            def _():
                act(remote(part.at[to], near.at[d], near_send.at[d], near_recv.at[d], device(y, to, z, core)))

    sums_x(lambda copy: copy.start())
    for d in range(1, NX):
        remote(near.at[d], near.at[d], near_send.at[d], near_recv.at[d], sibling).wait_recv()
    result = 0.5 * ((part[x] + near[1]) + (near[2] + near[3]))
    out_ref[pl.ds(0, 36, stride=2), :] = result[0:36]
    out_ref[pl.ds(1, 36, stride=2), :] = result[36:72]

    across.wait_send()
    for to in range(NZ):
        each_tile(to, lambda copy: copy.wait_send())
    for s in range(2 * NY):
        give(s).wait_send()
    own_copies(lambda copy: copy.wait_send())
    rest_copies(lambda copy: copy.wait_send())
    sums_x(lambda copy: copy.wait_send())


def body(amplitudes, integrals):
    left = jnp.transpose(amplitudes, (1, 2, 0)).reshape(48, 192)
    right = integrals.reshape(48, 256)
    dma = pltpu.SemaphoreType.DMA
    out = pl.pallas_call(
        kernel,
        out_shape=pltpu.VMEM((72, 128), jnp.float32),
        in_specs=[pl.BlockSpec(memory_space=pl.ANY)] * 2,
        out_specs=pl.BlockSpec(memory_space=pltpu.VMEM),
        scratch_shapes=[
            pltpu.VMEM((48, 192), jnp.bfloat16),
            pltpu.VMEM((2, 2, 48, 128), jnp.bfloat16),
            pltpu.VMEM((2, 2 * NY, 48, 128), jnp.bfloat16),
            pltpu.VMEM((2 * NY, 48, 256), jnp.bfloat16),
            pltpu.VMEM((NX, 72, 128), jnp.float32),
            pltpu.VMEM((NX, 72, 128), jnp.float32),
            dma((2,)), dma((2, NZ)), dma((2 * NY,)), dma((2 * NY,)), dma((2 * NY,)),
            dma((NY,)), dma((NY,)), dma((NY,)), dma((NY,)), dma((1,)), dma((1,)), dma((NX,)), dma((NX,)),
            pltpu.SemaphoreType.REGULAR((NZ,)), pltpu.SemaphoreType.REGULAR,
            pltpu.SemaphoreType.REGULAR((NY,)), pltpu.SemaphoreType.REGULAR((NX,)),
        ],
        compiler_params=pltpu.CompilerParams(collective_id=0, has_side_effects=True),
    )(left, right)
    return out.reshape(36, 1, 256)


def solution(mesh):
    return jax.shard_map(
        body,
        mesh=mesh,
        in_specs=(P("blk", None, "col"), P(None, "col", "blk")),
        out_specs=P("col", None, "blk"),
        check_vma=False,
    )
```

```python
import jax
import jax.numpy as jnp
from jax import lax
from jax.experimental import pallas as pl
from jax.experimental.pallas import tpu as pltpu
from jax.sharding import PartitionSpec as P

MESH = pl.DeviceIdType.MESH
NX, NY, NL, NZ = 4, 8, 6, 12
DEPTH = (48, 32)
RING_Y = (4, 3, 5, 2, 6, 1, 7)
ORDER_Y = (0, 1, 2, 3, 7, 6, 5, 4)


def device(y, x, z, core):
    return {"blk": (z % NL) * 2 + core, "col": (y * NX + x) * 2 + z // NL}


def remote(src, dst, send, recv, where):
    return pltpu.make_async_remote_copy(
        src_ref=src, dst_ref=dst, send_sem=send, recv_sem=recv, device_id=where, device_id_type=MESH
    )


def iotas():
    return lax.broadcasted_iota(jnp.int32, (192, 128), 1), lax.broadcasted_iota(jnp.int32, (192, 128), 0)


def chosen(hit):
    return jnp.where(hit, 1.0, 0.0).astype(jnp.bfloat16)


def wide_choice(block, to, half):
    lane, row = iotas()
    slot = (lane >= 40).astype(jnp.int32) + (lane >= 80).astype(jnp.int32) + (lane >= 120).astype(jnp.int32)
    inner = lane - 40 * slot
    source = 288 * to - 192 * block + 36 * half + 72 * (slot + lax.rem(to, 2)) + inner
    return chosen((source == row) & (inner < 36) & (slot < 3))


def narrow_choice(block, to, half, side):
    lane, row = iotas()
    lane = lane - 64 * side
    odd = lax.rem(to, 2)
    cut = 24 + 12 * odd
    slot = (lane >= cut).astype(jnp.int32)
    inner = jnp.where(lane >= cut, lane - cut, lane + 12 - 12 * odd)
    source = 288 * to - 192 * block + 36 * half + 72 * (slot + 2 - 2 * odd) + inner
    return chosen((source == row) & (lane >= 0) & (lane < 60))


def kernel(
    a_ref, b_ref, out_ref,
    a_own, tiles, a_all, b_all, part, near,
    local_sem, tile_send, tile_recv, pair_send, pair_recv,
    own_send, own_recv, rest_send, rest_recv, far_send, far_recv, near_send, near_recv, answer, answer_far, answer_y, answer_x,
):
    blk, col = lax.axis_index("blk"), lax.axis_index("col")
    zl, core = blk // 2, blk % 2
    zh, x, y = col % 2, (col // 2) % NX, col // (2 * NX)
    z = zh * NL + zl
    slot, other = zh * NY + y, (1 - zh) * NY + y

    load_a = pltpu.make_async_copy(a_ref, a_own, local_sem.at[0])
    load_b = pltpu.make_async_copy(b_ref, b_all.at[slot], local_sem.at[1])
    load_a.start()
    load_b.start()

    split = blk % 3 == 1
    targets = (2 * (blk // 3) + (blk % 3) // 2, 2 * (blk // 3) + 1)
    pair = y // 2
    kind = jnp.where(core == pair % 2, 0, 1)
    giver = jnp.where(kind == 0, (3 * pair + 2 * (y % 2)) // 2, (3 * pair + 1) // 2)
    gives_self = zl == giver
    sibling = device(y, x, z, 1 - core)

    barrier = pltpu.get_barrier_semaphore()

    def greet(where):
        pl.semaphore_signal(barrier, inc=1, device_id=where, device_id_type=MESH)

    def providers(half):
        return [device((y + d) % NY, x, half * NL + giver, core) for d in range(NY)]

    def signal(sem, where):
        pl.semaphore_signal(sem, inc=1, device_id=where, device_id_type=MESH)

    def rank(at):
        return jnp.where(at < 4, at, 11 - at)

    for d in range(1, NX):

        @pl.when((x + d) % NX > x)
        def _():
            greet(device(y, (x + d) % NX, z, core))

    for d in RING_Y:

        @pl.when(rank((y + d) % NY) > rank(y))
        def _():
            greet(device((y + d) % NY, x, z, core))

    greet(sibling)
    for half in (0, 1):

        @pl.when(half * NL + giver > z)
        def _():
            for where in providers(half):
                greet(where)

    for to in range(1, NZ):

        @pl.when(to > z)
        def _():
            greet(device(targets[0], x, to, core))

        @pl.when((to > z) & split)
        def _():
            greet(device(targets[1], x, to, core))

    @pl.when(z < NL)
    def _():
        greet(device(y, x, z + NL, core))

    per_plane = jnp.where(split, 2, 1)
    lower = jnp.where(giver < z, 1, 0) + jnp.where(NL + giver < z, 1, 0)
    partners = rank(y) + x + 1 + per_plane * z + NY * lower + jnp.where(z >= NL, 1, 0)
    pl.semaphore_wait(barrier, partners)

    across = remote(b_ref, b_all.at[slot], far_send.at[0], far_recv.at[0], device(y, x, (z + NL) % NZ, core))

    @pl.when(z >= NL)
    def _():
        signal(answer_far, device(y, x, z - NL, core))
        across.start()

    load_a.wait()
    mine = a_own[...]

    @pl.when(jnp.logical_not(split))
    def _():
        for half in range(2):
            tile = jnp.dot(mine, wide_choice(blk, targets[0], half), preferred_element_type=jnp.float32)
            tiles[0, half] = tile.astype(jnp.bfloat16)

    @pl.when(split)
    def _():
        for k in range(2):
            for half in range(2):
                low = jnp.dot(mine[0:32], narrow_choice(blk, targets[k], half, 0), preferred_element_type=jnp.float32)
                high = jnp.dot(mine[32:48], narrow_choice(blk, targets[k], half, 1), preferred_element_type=jnp.float32)
                tiles[k, half, 0:16] = (low[0:16] + high).astype(jnp.bfloat16)
                tiles[k, half, 16:32] = low[16:32].astype(jnp.bfloat16)

    def tile_copy(k, to, sort):
        return remote(
            tiles.at[k, to // NL, 0:DEPTH[sort]], a_all.at[sort, slot, 0:DEPTH[sort]], tile_send.at[k, to], tile_recv.at[slot],
            device(targets[k], x, to, core),
        )

    def each_tile(to, act):
        outside = [(to != z) | (targets[k] != y) for k in range(2)]

        @pl.when(outside[0] & jnp.logical_not(split))
        def _():
            act(tile_copy(0, to, 0))

        for k in range(2):

            @pl.when(outside[k] & split)
            def _():
                act(tile_copy(k, to, 1))

    def start_tiles(planes, low):
        for to in planes:

            @pl.when(to < z if low else to > z)
            def _():
                if not low:
                    pl.semaphore_wait(answer.at[to], per_plane)
                each_tile(to, lambda copy: copy.start())

    start_tiles(range(NZ - 1), True)
    for half in (0, 1):

        @pl.when(half * NL + giver < z)
        def _():
            for where in providers(half):
                signal(answer.at[z], where)

    for d in range(1, NY):

        @pl.when(rank((y + d) % NY) < rank(y))
        def _():
            signal(answer_y.at[NY - d], device((y + d) % NY, x, z, core))

    for d in range(1, NX):

        @pl.when((x + d) % NX < x)
        def _():
            signal(answer_x.at[NX - d], device(y, (x + d) % NX, z, core))

    for d in RING_Y:

        @pl.when(rank((y + d) % NY) > rank(y))
        def _():
            pl.semaphore_wait(answer_y.at[d], 1)

    def round_y(src, into, send, recv, act):
        for to in ORDER_Y:

            @pl.when(to != y)
            def _():
                act(remote(src, b_all.at[into], send.at[to], recv.at[y], device(to, x, z, core)))

    def own_copies(act):
        round_y(b_ref, slot, own_send, own_recv, act)

    def rest_copies(act):
        round_y(b_all.at[other], other, rest_send, rest_recv, act)

    def from_y(half, recv):
        for d in range(1, NY):
            at = (y + d) % NY
            block = b_all.at[half * NY + at]
            remote(block, block, own_send.at[0], recv.at[at], sibling).wait_recv()

    own_copies(lambda copy: copy.start())
    each_tile(z, lambda copy: copy.start())
    start_tiles(range(1, NL), False)

    @pl.when(z < NL)
    def _():
        pl.semaphore_wait(answer_far, 1)
        across.start()

    @pl.when(gives_self)
    def _():
        @pl.when(split)
        def _():
            a_all[1, slot, 0:32] = tiles[jnp.where(targets[1] == y, 1, 0), zh, 0:32]

        @pl.when(jnp.logical_not(split))
        def _():
            a_all[0, slot] = tiles[0, zh]

    across.wait_recv()
    rest_copies(lambda copy: copy.start())

    start_tiles(range(NL, NZ), False)

    def piece(sort, s):
        return a_all.at[sort, s, 0 : DEPTH[sort]]

    def arrival(sort, s):
        return remote(piece(sort, s), piece(sort, s), tile_send.at[0, 0], tile_recv.at[s], sibling)

    def give(sort, s):
        return remote(piece(sort, s), piece(sort, s), pair_send.at[s], pair_recv.at[s], sibling)

    for sort in range(2):

        @pl.when(kind == sort)
        def _():
            @pl.when(jnp.logical_not(gives_self))
            def _():
                arrival(sort, slot).wait_recv()

            give(sort, slot).start()
            for half in (zh, 1 - zh):
                for d in range(NY):
                    s = half * NY + (y + d) % NY
                    if d or half is not zh:
                        arrival(sort, s).wait_recv()
                        give(sort, s).start()
            for d in range(NY):
                give(1 - sort, zh * NY + d).wait_recv()

    load_b.wait()
    from_y(zh, own_recv)

    def matmul(sort, base, rows, first, last):
        left = a_all[sort, pl.ds(base, NY), 0:rows].reshape(NY * rows, 128)
        right = b_all[pl.ds(base, NY), first:last].reshape(NY * rows, 256)
        return lax.dot_general(left, right, (((0,), (0,)), ((), ())), preferred_element_type=jnp.float32)

    def product(sort, base):
        if sort == 0:
            return matmul(0, base, 48, 0, 48)
        return matmul(1, base, 32, 0, 32)[0:64] + matmul(1, base, 16, 32, 48)[64:128]

    base, far_base = zh * NY, (1 - zh) * NY
    wide, narrow = product(0, base), product(1, base)
    for sort in range(2):

        @pl.when(kind == sort)
        def _():
            for d in range(NY):
                give(1 - sort, (1 - zh) * NY + d).wait_recv()

    from_y(1 - zh, rest_recv)
    wide += product(0, far_base)
    narrow += product(1, far_base)
    w = [wide[40 * i : 40 * i + 36] for i in range(3)]
    odd = y % 2 == 1
    none = jnp.zeros((12, 256), jnp.float32)
    n = [
        jnp.where(odd, narrow[0:36], jnp.concatenate([none, narrow[0:24]], axis=0)),
        jnp.where(odd, jnp.concatenate([narrow[36:60], none], axis=0), narrow[24:60]),
    ]
    sums = (
        jnp.where(odd, n[0], w[0]),
        jnp.where(odd, n[1] + w[0], w[1]),
        jnp.where(odd, w[1], w[2] + n[0]),
        jnp.where(odd, w[2], n[1]),
    )
    for i, value in enumerate(sums):
        part[i, 0:36] = value[:, 0:128]
        part[i, 36:72] = value[:, 128:256]

    for d in range(1, NX):

        @pl.when((x + d) % NX > x)
        def _():
            pl.semaphore_wait(answer_x.at[d], 1)

    def sums_x(act):
        for to in range(NX):
            d = jnp.where(to > x, to - x, to - x + NX)

            @pl.when(to != x)
            def _():
                act(remote(part.at[to], near.at[d], near_send.at[d], near_recv.at[d], device(y, to, z, core)))

    sums_x(lambda copy: copy.start())
    for d in range(1, NX):
        remote(near.at[d], near.at[d], near_send.at[d], near_recv.at[d], sibling).wait_recv()
    result = 0.5 * ((part[x] + near[1]) + (near[2] + near[3]))
    out_ref[pl.ds(0, 36, stride=2), :] = result[0:36]
    out_ref[pl.ds(1, 36, stride=2), :] = result[36:72]

    across.wait_send()
    for to in range(NZ):
        each_tile(to, lambda copy: copy.wait_send())
    for sort in range(2):

        @pl.when(kind == sort)
        def _():
            for s in range(2 * NY):
                give(sort, s).wait_send()

    own_copies(lambda copy: copy.wait_send())
    rest_copies(lambda copy: copy.wait_send())
    sums_x(lambda copy: copy.wait_send())


def body(amplitudes, integrals):
    left = jnp.transpose(amplitudes, (1, 2, 0)).reshape(48, 192)
    right = integrals.reshape(48, 256)
    dma = pltpu.SemaphoreType.DMA
    out = pl.pallas_call(
        kernel,
        out_shape=pltpu.VMEM((72, 128), jnp.float32),
        in_specs=[pl.BlockSpec(memory_space=pl.ANY)] * 2,
        out_specs=pl.BlockSpec(memory_space=pltpu.VMEM),
        scratch_shapes=[
            pltpu.VMEM((48, 192), jnp.bfloat16),
            pltpu.VMEM((2, 2, 48, 128), jnp.bfloat16),
            pltpu.VMEM((2, 2 * NY, 48, 128), jnp.bfloat16),
            pltpu.VMEM((2 * NY, 48, 256), jnp.bfloat16),
            pltpu.VMEM((NX, 72, 128), jnp.float32),
            pltpu.VMEM((NX, 72, 128), jnp.float32),
            dma((2,)), dma((2, NZ)), dma((2 * NY,)), dma((2 * NY,)), dma((2 * NY,)),
            dma((NY,)), dma((NY,)), dma((NY,)), dma((NY,)), dma((1,)), dma((1,)), dma((NX,)), dma((NX,)),
            pltpu.SemaphoreType.REGULAR((NZ,)), pltpu.SemaphoreType.REGULAR,
            pltpu.SemaphoreType.REGULAR((NY,)), pltpu.SemaphoreType.REGULAR((NX,)),
        ],
        compiler_params=pltpu.CompilerParams(collective_id=0, has_side_effects=True),
    )(left, right)
    return out.reshape(36, 1, 256)


def solution(mesh):
    return jax.shard_map(
        body,
        mesh=mesh,
        in_specs=(P("blk", None, "col"), P(None, "col", "blk")),
        out_specs=P("col", None, "blk"),
        check_vma=False,
    )
```

```python
import jax
import jax.numpy as jnp
from jax import lax
from jax.experimental import pallas as pl
from jax.experimental.pallas import tpu as pltpu
from jax.sharding import PartitionSpec as P

MESH = pl.DeviceIdType.MESH
NX, NY, NL, NZ = 4, 8, 6, 12
DEPTH = (48, 32)
RING_Y = (4, 3, 5, 2, 6, 1, 7)
ORDER_Y = (0, 1, 2, 3, 7, 6, 5, 4)


def device(y, x, z, core):
    return {"blk": (z % NL) * 2 + core, "col": (y * NX + x) * 2 + z // NL}


def remote(src, dst, send, recv, where):
    return pltpu.make_async_remote_copy(
        src_ref=src, dst_ref=dst, send_sem=send, recv_sem=recv, device_id=where, device_id_type=MESH
    )


def iotas():
    return lax.broadcasted_iota(jnp.int32, (192, 128), 1), lax.broadcasted_iota(jnp.int32, (192, 128), 0)


def chosen(hit):
    return jnp.where(hit, 1.0, 0.0).astype(jnp.bfloat16)


def wide_choice(block, to, half):
    lane, row = iotas()
    slot = (lane >= 40).astype(jnp.int32) + (lane >= 80).astype(jnp.int32) + (lane >= 120).astype(jnp.int32)
    inner = lane - 40 * slot
    source = 288 * to - 192 * block + 36 * half + 72 * (slot + lax.rem(to, 2)) + inner
    return chosen((source == row) & (inner < 36) & (slot < 3))


def narrow_choice(block, to, half, side):
    lane, row = iotas()
    lane = lane - 64 * side
    odd = lax.rem(to, 2)
    cut = 24 + 12 * odd
    slot = (lane >= cut).astype(jnp.int32)
    inner = jnp.where(lane >= cut, lane - cut, lane + 12 - 12 * odd)
    source = 288 * to - 192 * block + 36 * half + 72 * (slot + 2 - 2 * odd) + inner
    return chosen((source == row) & (lane >= 0) & (lane < 60))


def kernel(
    a_ref, b_ref, out_ref,
    a_own, tiles, a_all, b_all, part, near,
    local_sem, tile_send, tile_recv, pair_send, pair_recv,
    own_send, own_recv, rest_send, rest_recv, far_send, far_recv, near_send, near_recv, answer, answer_far, answer_y, answer_x,
):
    blk, col = lax.axis_index("blk"), lax.axis_index("col")
    zl, core = blk // 2, blk % 2
    zh, x, y = col % 2, (col // 2) % NX, col // (2 * NX)
    z = zh * NL + zl
    slot, other = zh * NY + y, (1 - zh) * NY + y

    load_a = pltpu.make_async_copy(a_ref, a_own, local_sem.at[0])
    load_b = pltpu.make_async_copy(b_ref, b_all.at[slot], local_sem.at[1])
    load_b.start()
    load_a.start()

    split = blk % 3 == 1
    targets = (2 * (blk // 3) + (blk % 3) // 2, 2 * (blk // 3) + 1)
    pair = y // 2
    kind = jnp.where(core == pair % 2, 0, 1)
    giver = jnp.where(kind == 0, (3 * pair + 2 * (y % 2)) // 2, (3 * pair + 1) // 2)
    gives_self = zl == giver
    sibling = device(y, x, z, 1 - core)

    barrier = pltpu.get_barrier_semaphore()

    def greet(where):
        pl.semaphore_signal(barrier, inc=1, device_id=where, device_id_type=MESH)

    def providers(half):
        return [device((y + d) % NY, x, half * NL + giver, core) for d in range(NY)]

    def signal(sem, where):
        pl.semaphore_signal(sem, inc=1, device_id=where, device_id_type=MESH)

    def rank(at):
        return jnp.where(at < 4, at, 11 - at)

    for d in range(1, NX):

        @pl.when((x + d) % NX > x)
        def _():
            greet(device(y, (x + d) % NX, z, core))

    for d in RING_Y:

        @pl.when(rank((y + d) % NY) > rank(y))
        def _():
            greet(device((y + d) % NY, x, z, core))

    greet(sibling)
    for half in (0, 1):

        @pl.when(half * NL + giver > z)
        def _():
            for where in providers(half):
                greet(where)

    for to in range(1, NZ):

        @pl.when(to > z)
        def _():
            greet(device(targets[0], x, to, core))

        @pl.when((to > z) & split)
        def _():
            greet(device(targets[1], x, to, core))

    @pl.when(z < NL)
    def _():
        greet(device(y, x, z + NL, core))

    per_plane = jnp.where(split, 2, 1)
    lower = jnp.where(giver < z, 1, 0) + jnp.where(NL + giver < z, 1, 0)
    partners = rank(y) + x + 1 + per_plane * z + NY * lower + jnp.where(z >= NL, 1, 0)
    pl.semaphore_wait(barrier, partners)

    load_b.wait()
    across = remote(b_all.at[slot], b_all.at[slot], far_send.at[0], far_recv.at[0], device(y, x, (z + NL) % NZ, core))

    @pl.when(z >= NL)
    def _():
        signal(answer_far, device(y, x, z - NL, core))
        across.start()

    load_a.wait()
    mine = a_own[...]

    @pl.when(jnp.logical_not(split))
    def _():
        for half in range(2):
            tile = jnp.dot(mine, wide_choice(blk, targets[0], half), preferred_element_type=jnp.float32)
            tiles[0, half] = tile.astype(jnp.bfloat16)

    @pl.when(split)
    def _():
        for k in range(2):
            for half in range(2):
                low = jnp.dot(mine[0:32], narrow_choice(blk, targets[k], half, 0), preferred_element_type=jnp.float32)
                high = jnp.dot(mine[32:48], narrow_choice(blk, targets[k], half, 1), preferred_element_type=jnp.float32)
                tiles[k, half, 0:16] = (low[0:16] + high).astype(jnp.bfloat16)
                tiles[k, half, 16:32] = low[16:32].astype(jnp.bfloat16)

    def tile_copy(k, to, sort):
        return remote(
            tiles.at[k, to // NL, 0:DEPTH[sort]], a_all.at[sort, slot, 0:DEPTH[sort]], tile_send.at[k, to], tile_recv.at[slot],
            device(targets[k], x, to, core),
        )

    def each_tile(to, act):
        outside = [(to != z) | (targets[k] != y) for k in range(2)]

        @pl.when(outside[0] & jnp.logical_not(split))
        def _():
            act(tile_copy(0, to, 0))

        for k in range(2):

            @pl.when(outside[k] & split)
            def _():
                act(tile_copy(k, to, 1))

    def start_tiles(planes, low):
        for to in planes:

            @pl.when(to < z if low else to > z)
            def _():
                if not low:
                    pl.semaphore_wait(answer.at[to], per_plane)
                each_tile(to, lambda copy: copy.start())

    start_tiles(range(NZ - 1), True)
    for half in (0, 1):

        @pl.when(half * NL + giver < z)
        def _():
            for where in providers(half):
                signal(answer.at[z], where)

    for d in range(1, NY):

        @pl.when(rank((y + d) % NY) < rank(y))
        def _():
            signal(answer_y.at[NY - d], device((y + d) % NY, x, z, core))

    for d in range(1, NX):

        @pl.when((x + d) % NX < x)
        def _():
            signal(answer_x.at[NX - d], device(y, (x + d) % NX, z, core))

    for d in RING_Y:

        @pl.when(rank((y + d) % NY) > rank(y))
        def _():
            pl.semaphore_wait(answer_y.at[d], 1)

    def round_y(src, into, send, recv, act):
        for to in ORDER_Y:

            @pl.when(to != y)
            def _():
                act(remote(src, b_all.at[into], send.at[to], recv.at[y], device(to, x, z, core)))

    def own_copies(act):
        round_y(b_all.at[slot], slot, own_send, own_recv, act)

    def rest_copies(act):
        round_y(b_all.at[other], other, rest_send, rest_recv, act)

    def from_y(half, recv):
        for d in range(1, NY):
            at = (y + d) % NY
            block = b_all.at[half * NY + at]
            remote(block, block, own_send.at[0], recv.at[at], sibling).wait_recv()

    own_copies(lambda copy: copy.start())
    each_tile(z, lambda copy: copy.start())
    start_tiles(range(1, NL), False)

    @pl.when(z < NL)
    def _():
        pl.semaphore_wait(answer_far, 1)
        across.start()

    @pl.when(gives_self)
    def _():
        @pl.when(split)
        def _():
            a_all[1, slot, 0:32] = tiles[jnp.where(targets[1] == y, 1, 0), zh, 0:32]

        @pl.when(jnp.logical_not(split))
        def _():
            a_all[0, slot] = tiles[0, zh]

    across.wait_recv()
    rest_copies(lambda copy: copy.start())

    start_tiles(range(NL, NZ), False)

    def piece(sort, s):
        return a_all.at[sort, s, 0 : DEPTH[sort]]

    def arrival(sort, s):
        return remote(piece(sort, s), piece(sort, s), tile_send.at[0, 0], tile_recv.at[s], sibling)

    def give(sort, s):
        return remote(piece(sort, s), piece(sort, s), pair_send.at[s], pair_recv.at[s], sibling)

    for sort in range(2):

        @pl.when(kind == sort)
        def _():
            @pl.when(jnp.logical_not(gives_self))
            def _():
                arrival(sort, slot).wait_recv()

            give(sort, slot).start()
            for half in (zh, 1 - zh):
                for d in range(NY):
                    s = half * NY + (y + d) % NY
                    if d or half is not zh:
                        arrival(sort, s).wait_recv()
                        give(sort, s).start()
            for d in range(NY):
                give(1 - sort, zh * NY + d).wait_recv()

    from_y(zh, own_recv)

    def matmul(sort, base, rows, first, last):
        left = a_all[sort, pl.ds(base, NY), 0:rows].reshape(NY * rows, 128)
        right = b_all[pl.ds(base, NY), first:last].reshape(NY * rows, 256)
        return lax.dot_general(left, right, (((0,), (0,)), ((), ())), preferred_element_type=jnp.float32)

    def product(sort, base):
        if sort == 0:
            return matmul(0, base, 48, 0, 48)
        return matmul(1, base, 32, 0, 32)[0:64] + matmul(1, base, 16, 32, 48)[64:128]

    base, far_base = zh * NY, (1 - zh) * NY
    wide, narrow = product(0, base), product(1, base)
    for sort in range(2):

        @pl.when(kind == sort)
        def _():
            for d in range(NY):
                give(1 - sort, (1 - zh) * NY + d).wait_recv()

    from_y(1 - zh, rest_recv)
    wide += product(0, far_base)
    narrow += product(1, far_base)
    w = [wide[40 * i : 40 * i + 36] for i in range(3)]
    odd = y % 2 == 1
    none = jnp.zeros((12, 256), jnp.float32)
    n = [
        jnp.where(odd, narrow[0:36], jnp.concatenate([none, narrow[0:24]], axis=0)),
        jnp.where(odd, jnp.concatenate([narrow[36:60], none], axis=0), narrow[24:60]),
    ]
    sums = (
        jnp.where(odd, n[0], w[0]),
        jnp.where(odd, n[1] + w[0], w[1]),
        jnp.where(odd, w[1], w[2] + n[0]),
        jnp.where(odd, w[2], n[1]),
    )
    for i, value in enumerate(sums):
        part[i, 0:36] = value[:, 0:128]
        part[i, 36:72] = value[:, 128:256]

    for d in range(1, NX):

        @pl.when((x + d) % NX > x)
        def _():
            pl.semaphore_wait(answer_x.at[d], 1)

    def sums_x(act):
        for to in range(NX):
            d = jnp.where(to > x, to - x, to - x + NX)

            @pl.when(to != x)
            def _():
                act(remote(part.at[to], near.at[d], near_send.at[d], near_recv.at[d], device(y, to, z, core)))

    sums_x(lambda copy: copy.start())
    for d in range(1, NX):
        remote(near.at[d], near.at[d], near_send.at[d], near_recv.at[d], sibling).wait_recv()
    result = 0.5 * ((part[x] + near[1]) + (near[2] + near[3]))
    out_ref[pl.ds(0, 36, stride=2), :] = result[0:36]
    out_ref[pl.ds(1, 36, stride=2), :] = result[36:72]

    across.wait_send()
    for to in range(NZ):
        each_tile(to, lambda copy: copy.wait_send())
    for sort in range(2):

        @pl.when(kind == sort)
        def _():
            for s in range(2 * NY):
                give(sort, s).wait_send()

    own_copies(lambda copy: copy.wait_send())
    rest_copies(lambda copy: copy.wait_send())
    sums_x(lambda copy: copy.wait_send())


def body(amplitudes, integrals):
    left = jnp.transpose(amplitudes, (1, 2, 0)).reshape(48, 192)
    right = integrals.reshape(48, 256)
    dma = pltpu.SemaphoreType.DMA
    out = pl.pallas_call(
        kernel,
        out_shape=pltpu.VMEM((72, 128), jnp.float32),
        in_specs=[pl.BlockSpec(memory_space=pl.ANY)] * 2,
        out_specs=pl.BlockSpec(memory_space=pltpu.VMEM),
        scratch_shapes=[
            pltpu.VMEM((48, 192), jnp.bfloat16),
            pltpu.VMEM((2, 2, 48, 128), jnp.bfloat16),
            pltpu.VMEM((2, 2 * NY, 48, 128), jnp.bfloat16),
            pltpu.VMEM((2 * NY, 48, 256), jnp.bfloat16),
            pltpu.VMEM((NX, 72, 128), jnp.float32),
            pltpu.VMEM((NX, 72, 128), jnp.float32),
            dma((2,)), dma((2, NZ)), dma((2 * NY,)), dma((2 * NY,)), dma((2 * NY,)),
            dma((NY,)), dma((NY,)), dma((NY,)), dma((NY,)), dma((1,)), dma((1,)), dma((NX,)), dma((NX,)),
            pltpu.SemaphoreType.REGULAR((NZ,)), pltpu.SemaphoreType.REGULAR,
            pltpu.SemaphoreType.REGULAR((NY,)), pltpu.SemaphoreType.REGULAR((NX,)),
        ],
        compiler_params=pltpu.CompilerParams(collective_id=0, has_side_effects=True),
    )(left, right)
    return out.reshape(36, 1, 256)


def solution(mesh):
    return jax.shard_map(
        body,
        mesh=mesh,
        in_specs=(P("blk", None, "col"), P(None, "col", "blk")),
        out_specs=P("col", None, "blk"),
        check_vma=False,
    )
```

```python
import jax
import jax.numpy as jnp
from jax import lax
from jax.experimental import pallas as pl
from jax.experimental.pallas import tpu as pltpu
from jax.sharding import PartitionSpec as P

MESH = pl.DeviceIdType.MESH
NX, NY, NL, NZ = 4, 8, 6, 12
DEPTH = (48, 32)
RING_Y = (4, 3, 5, 2, 6, 1, 7)
ORDER_Y = (0, 1, 2, 3, 7, 6, 5, 4)


def device(y, x, z, core):
    return {"blk": (z % NL) * 2 + core, "col": (y * NX + x) * 2 + z // NL}


def remote(src, dst, send, recv, where):
    return pltpu.make_async_remote_copy(
        src_ref=src, dst_ref=dst, send_sem=send, recv_sem=recv, device_id=where, device_id_type=MESH
    )


def iotas():
    return lax.broadcasted_iota(jnp.int32, (192, 128), 1), lax.broadcasted_iota(jnp.int32, (192, 128), 0)


def chosen(hit):
    return jnp.where(hit, 1.0, 0.0).astype(jnp.bfloat16)


def wide_choice(block, to, half):
    lane, row = iotas()
    slot = (lane >= 40).astype(jnp.int32) + (lane >= 80).astype(jnp.int32) + (lane >= 120).astype(jnp.int32)
    inner = lane - 40 * slot
    source = 288 * to - 192 * block + 36 * half + 72 * (slot + lax.rem(to, 2)) + inner
    return chosen((source == row) & (inner < 36) & (slot < 3))


def narrow_choice(block, to, half, side):
    lane, row = iotas()
    lane = lane - 64 * side
    odd = lax.rem(to, 2)
    cut = 24 + 12 * odd
    slot = (lane >= cut).astype(jnp.int32)
    inner = jnp.where(lane >= cut, lane - cut, lane + 12 - 12 * odd)
    source = 288 * to - 192 * block + 36 * half + 72 * (slot + 2 - 2 * odd) + inner
    return chosen((source == row) & (lane >= 0) & (lane < 60))


def kernel(
    a_ref, b_ref, out_ref,
    a_own, tiles, a_all, b_all, part, near,
    local_sem, tile_send, tile_recv, pair_send, pair_recv,
    own_send, own_recv, rest_send, rest_recv, far_send, far_recv, near_send, near_recv, answer, answer_far, answer_y, answer_x,
):
    blk, col = lax.axis_index("blk"), lax.axis_index("col")
    zl, core = blk // 2, blk % 2
    zh, x, y = col % 2, (col // 2) % NX, col // (2 * NX)
    z = zh * NL + zl
    slot, other = zh * NY + y, (1 - zh) * NY + y

    load_a = pltpu.make_async_copy(a_ref, a_own, local_sem.at[0])
    load_b = pltpu.make_async_copy(b_ref, b_all.at[slot], local_sem.at[1])
    load_b.start()
    load_a.start()

    split = blk % 3 == 1
    targets = (2 * (blk // 3) + (blk % 3) // 2, 2 * (blk // 3) + 1)
    pair = y // 2
    kind = jnp.where(core == pair % 2, 0, 1)
    giver = jnp.where(kind == 0, (3 * pair + 2 * (y % 2)) // 2, (3 * pair + 1) // 2)
    gives_self = zl == giver
    sibling = device(y, x, z, 1 - core)

    barrier = pltpu.get_barrier_semaphore()

    def greet(where):
        pl.semaphore_signal(barrier, inc=1, device_id=where, device_id_type=MESH)

    def providers(half):
        return [device((y + d) % NY, x, half * NL + giver, core) for d in range(NY)]

    def signal(sem, where):
        pl.semaphore_signal(sem, inc=1, device_id=where, device_id_type=MESH)

    def rank(at):
        return jnp.where(at < 4, at, 11 - at)

    for d in range(1, NX):

        @pl.when((x + d) % NX > x)
        def _():
            greet(device(y, (x + d) % NX, z, core))

    for d in RING_Y:

        @pl.when(rank((y + d) % NY) > rank(y))
        def _():
            greet(device((y + d) % NY, x, z, core))

    greet(sibling)
    for half in (0, 1):

        @pl.when(half * NL + giver > z)
        def _():
            for where in providers(half):
                greet(where)

    for to in range(1, NZ):

        @pl.when(to > z)
        def _():
            greet(device(targets[0], x, to, core))

        @pl.when((to > z) & split)
        def _():
            greet(device(targets[1], x, to, core))

    @pl.when(z < NL)
    def _():
        greet(device(y, x, z + NL, core))

    per_plane = jnp.where(split, 2, 1)
    lower = jnp.where(giver < z, 1, 0) + jnp.where(NL + giver < z, 1, 0)
    partners = rank(y) + x + 1 + per_plane * z + NY * lower + jnp.where(z >= NL, 1, 0)
    pl.semaphore_wait(barrier, partners)

    load_b.wait()
    across = remote(b_all.at[slot], b_all.at[slot], far_send.at[0], far_recv.at[0], device(y, x, (z + NL) % NZ, core))

    @pl.when(z >= NL)
    def _():
        signal(answer_far, device(y, x, z - NL, core))
        across.start()

    load_a.wait()
    mine = a_own[...]

    @pl.when(jnp.logical_not(split))
    def _():
        for half in range(2):
            tile = jnp.dot(mine, wide_choice(blk, targets[0], half), preferred_element_type=jnp.float32)
            tiles[0, half] = tile.astype(jnp.bfloat16)

    @pl.when(split)
    def _():
        for k in range(2):
            for half in range(2):
                low = jnp.dot(mine[0:32], narrow_choice(blk, targets[k], half, 0), preferred_element_type=jnp.float32)
                high = jnp.dot(mine[32:48], narrow_choice(blk, targets[k], half, 1), preferred_element_type=jnp.float32)
                tiles[k, half, 0:16] = (low[0:16] + high).astype(jnp.bfloat16)
                tiles[k, half, 16:32] = low[16:32].astype(jnp.bfloat16)

    def tile_copy(k, to, sort):
        return remote(
            tiles.at[k, to // NL, 0:DEPTH[sort]], a_all.at[sort, slot, 0:DEPTH[sort]], tile_send.at[k, to], tile_recv.at[slot],
            device(targets[k], x, to, core),
        )

    def each_tile(to, act):
        outside = [(to != z) | (targets[k] != y) for k in range(2)]

        @pl.when(outside[0] & jnp.logical_not(split))
        def _():
            act(tile_copy(0, to, 0))

        for k in range(2):

            @pl.when(outside[k] & split)
            def _():
                act(tile_copy(k, to, 1))

    def start_tiles(planes, low):
        for to in planes:

            @pl.when(to < z if low else to > z)
            def _():
                if not low:
                    pl.semaphore_wait(answer.at[to], per_plane)
                each_tile(to, lambda copy: copy.start())

    start_tiles(range(NZ - 1), True)
    for half in (0, 1):

        @pl.when(half * NL + giver < z)
        def _():
            for where in providers(half):
                signal(answer.at[z], where)

    for d in range(1, NY):

        @pl.when(rank((y + d) % NY) < rank(y))
        def _():
            signal(answer_y.at[NY - d], device((y + d) % NY, x, z, core))

    for d in range(1, NX):

        @pl.when((x + d) % NX < x)
        def _():
            signal(answer_x.at[NX - d], device(y, (x + d) % NX, z, core))

    for d in RING_Y:

        @pl.when(rank((y + d) % NY) > rank(y))
        def _():
            pl.semaphore_wait(answer_y.at[d], 1)

    def round_y(src, into, send, recv, act):
        for to in ORDER_Y:

            @pl.when(to != y)
            def _():
                act(remote(src, b_all.at[into], send.at[to], recv.at[y], device(to, x, z, core)))

    def own_copies(act):
        round_y(b_all.at[slot], slot, own_send, own_recv, act)

    def rest_copies(act):
        round_y(b_all.at[other], other, rest_send, rest_recv, act)

    def from_y(half, recv):
        for d in range(1, NY):
            at = (y + d) % NY
            block = b_all.at[half * NY + at]
            remote(block, block, own_send.at[0], recv.at[at], sibling).wait_recv()

    own_copies(lambda copy: copy.start())
    each_tile(z, lambda copy: copy.start())
    start_tiles(range(1, NL), False)

    @pl.when(z < NL)
    def _():
        pl.semaphore_wait(answer_far, 1)
        across.start()

    @pl.when(gives_self)
    def _():
        @pl.when(split)
        def _():
            a_all[1, slot, 0:32] = tiles[jnp.where(targets[1] == y, 1, 0), zh, 0:32]

        @pl.when(jnp.logical_not(split))
        def _():
            a_all[0, slot] = tiles[0, zh]

    across.wait_recv()
    rest_copies(lambda copy: copy.start())

    start_tiles(range(NL, NZ), False)

    def piece(sort, s):
        return a_all.at[sort, s, 0 : DEPTH[sort]]

    def arrival(sort, s):
        return remote(piece(sort, s), piece(sort, s), tile_send.at[0, 0], tile_recv.at[s], sibling)

    def give(sort, s):
        return remote(piece(sort, s), piece(sort, s), pair_send.at[s], pair_recv.at[s], sibling)

    for sort in range(2):

        @pl.when(kind == sort)
        def _():
            @pl.when(jnp.logical_not(gives_self))
            def _():
                arrival(sort, slot).wait_recv()

            give(sort, slot).start()
            for half in (zh, 1 - zh):
                for d in range(NY):
                    s = half * NY + (y + d) % NY
                    if d or half is not zh:
                        arrival(sort, s).wait_recv()
                        give(sort, s).start()
            for d in range(NY):
                give(1 - sort, zh * NY + d).wait_recv()

    from_y(zh, own_recv)

    def matmul(sort, base, rows, first, last):
        left = a_all[sort, pl.ds(base, NY), 0:rows].reshape(NY * rows, 128)
        right = b_all[pl.ds(base, NY), first:last].reshape(NY * rows, 256)
        return lax.dot_general(left, right, (((0,), (0,)), ((), ())), preferred_element_type=jnp.float32)

    def product(sort, base):
        if sort == 0:
            return matmul(0, base, 48, 0, 48)
        return matmul(1, base, 32, 0, 32)[0:64] + matmul(1, base, 16, 32, 48)[64:128]

    for d in range(1, NX):

        @pl.when((x + d) % NX > x)
        def _():
            pl.semaphore_wait(answer_x.at[d], 1)

    base, far_base = zh * NY, (1 - zh) * NY
    wide, narrow = product(0, base), product(1, base)
    for sort in range(2):

        @pl.when(kind == sort)
        def _():
            for d in range(NY):
                give(1 - sort, (1 - zh) * NY + d).wait_recv()

    from_y(1 - zh, rest_recv)
    wide += product(0, far_base)
    narrow += product(1, far_base)
    w = [wide[40 * i : 40 * i + 36] for i in range(3)]
    odd = y % 2 == 1
    none = jnp.zeros((12, 256), jnp.float32)
    n = [
        jnp.where(odd, narrow[0:36], jnp.concatenate([none, narrow[0:24]], axis=0)),
        jnp.where(odd, jnp.concatenate([narrow[36:60], none], axis=0), narrow[24:60]),
    ]
    sums = (
        jnp.where(odd, n[0], w[0]),
        jnp.where(odd, n[1] + w[0], w[1]),
        jnp.where(odd, w[1], w[2] + n[0]),
        jnp.where(odd, w[2], n[1]),
    )
    for i, value in enumerate(sums):
        part[i, 0:36] = value[:, 0:128]
        part[i, 36:72] = value[:, 128:256]

    def sums_x(act):
        for to in range(NX):
            d = jnp.where(to > x, to - x, to - x + NX)

            @pl.when(to != x)
            def _():
                act(remote(part.at[to], near.at[d], near_send.at[d], near_recv.at[d], device(y, to, z, core)))

    sums_x(lambda copy: copy.start())
    for d in range(1, NX):
        remote(near.at[d], near.at[d], near_send.at[d], near_recv.at[d], sibling).wait_recv()
    result = 0.5 * ((part[x] + near[1]) + (near[2] + near[3]))
    out_ref[pl.ds(0, 36, stride=2), :] = result[0:36]
    out_ref[pl.ds(1, 36, stride=2), :] = result[36:72]

    across.wait_send()
    for to in range(NZ):
        each_tile(to, lambda copy: copy.wait_send())
    for sort in range(2):

        @pl.when(kind == sort)
        def _():
            for s in range(2 * NY):
                give(sort, s).wait_send()

    own_copies(lambda copy: copy.wait_send())
    rest_copies(lambda copy: copy.wait_send())
    sums_x(lambda copy: copy.wait_send())


def body(amplitudes, integrals):
    left = jnp.transpose(amplitudes, (1, 2, 0)).reshape(48, 192)
    right = integrals.reshape(48, 256)
    dma = pltpu.SemaphoreType.DMA
    out = pl.pallas_call(
        kernel,
        out_shape=pltpu.VMEM((72, 128), jnp.float32),
        in_specs=[pl.BlockSpec(memory_space=pl.ANY)] * 2,
        out_specs=pl.BlockSpec(memory_space=pltpu.VMEM),
        scratch_shapes=[
            pltpu.VMEM((48, 192), jnp.bfloat16),
            pltpu.VMEM((2, 2, 48, 128), jnp.bfloat16),
            pltpu.VMEM((2, 2 * NY, 48, 128), jnp.bfloat16),
            pltpu.VMEM((2 * NY, 48, 256), jnp.bfloat16),
            pltpu.VMEM((NX, 72, 128), jnp.float32),
            pltpu.VMEM((NX, 72, 128), jnp.float32),
            dma((2,)), dma((2, NZ)), dma((2 * NY,)), dma((2 * NY,)), dma((2 * NY,)),
            dma((NY,)), dma((NY,)), dma((NY,)), dma((NY,)), dma((1,)), dma((1,)), dma((NX,)), dma((NX,)),
            pltpu.SemaphoreType.REGULAR((NZ,)), pltpu.SemaphoreType.REGULAR,
            pltpu.SemaphoreType.REGULAR((NY,)), pltpu.SemaphoreType.REGULAR((NX,)),
        ],
        compiler_params=pltpu.CompilerParams(collective_id=0, has_side_effects=True),
    )(left, right)
    return out.reshape(36, 1, 256)


def solution(mesh):
    return jax.shard_map(
        body,
        mesh=mesh,
        in_specs=(P("blk", None, "col"), P(None, "col", "blk")),
        out_specs=P("col", None, "blk"),
        check_vma=False,
    )
```
